32 devices in a mesh: dev: 32 (over z, y, x, core).
Axes of the slice: x: 2, y: 2, z: 4, core: 2. Of those that a mesh axis runs over, the one named last changes fastest.
Arguments:
- log_depth: float32 [256, 12544], P('dev'), may hold values from -1.5 to 1.5
- depth_m: float32 [256, 12544], P('dev'), may hold values from -0.006 to 0.006
- depth_v: float32 [256, 12544], P('dev'), may hold values from 1e-07 to 1e-05
- image_params: float32 [7, 256], P(None, 'dev'), may hold values from -1.5 to 1.5
- image_m: float32 [7, 256], P(None, 'dev'), may hold values from -6 to 6
- image_v: float32 [7, 256], P(None, 'dev'), may hold values from 0.1 to 10
- pair_points: bfloat16 [768, 2, 3, 12544], P('dev'), may hold values from -6 to 6
- pair_conf: bfloat16 [768, 2, 12544], P('dev'), may hold values from 1 to 5
- pair_params: float32 [7, 768], P(None, 'dev'), may hold values from -1.5 to 1.5
- pair_m: float32 [7, 768], P(None, 'dev'), may hold values from -6 to 6
- pair_v: float32 [7, 768], P(None, 'dev'), may hold values from 0.1 to 10
- fetch: int32 [32, 9], P('dev'), may hold values from 0 to 7
- pair_sides: int32 [768, 2], P('dev'), may hold values from 0 to 8, as said below
- pair_count: int32 [32], P('dev'), may hold values from 6 to 24, as said below
Outputs:
- new_depth: float32 [256, 12544], P('dev')
- new_image_params: float32 [7, 256], P(None, 'dev')
- new_pair_params: float32 [7, 768], P(None, 'dev')
The draws below stay inside these ranges and needn't reach their ends.
Inputs may be any that keep to these rules, and one draw needn't show every extreme that they name: `pair_sides`: the two positions of a slot differ. The first slot of every holder has second position 8. `pair_count`: each holder has at least a quarter of its slots live, and some holder has all 24 live.
All inputs are finite; a program needn't handle non-finite values.
Results may differ from the reference program's by a relative error of at most 0.0003.
Values may be sent and summed in bfloat16 or wider, within the bound.
A program may use at most 128 MiB of HBM per device.

```python
import math
import jax
import jax.numpy as jnp
from jax import lax

IMG_SIDE = 112
PIX = 12544
IMG_DEV = 8
SLOTS = 24
REACH = 4
ITERS = 2
HOLDERS = 32
IMAGES = 256
PAIRS = 768


def draw_pair_sides(key, part):
    width_k = 2 * REACH + 1
    first_key = jax.random.fold_in(key, 11)
    second_key = jax.random.fold_in(key, 12)
    lead_key = jax.random.fold_in(key, 13)
    first = jax.random.randint(first_key, (PAIRS,), 0, width_k)
    stride = jax.random.randint(second_key, (PAIRS,), 1, width_k)
    second = (first + stride) % width_k
    lead_first = jax.random.randint(lead_key, (PAIRS,), 0, width_k - 1)
    is_lead = jnp.arange(PAIRS) % SLOTS == 0
    first = jnp.where(is_lead, lead_first, first)
    second = jnp.where(is_lead, width_k - 1, second)
    return jnp.stack([first, second], axis=1).astype(jnp.int32)


def draw_pair_count(key, part):
    count_key = jax.random.fold_in(key, 21)
    full_key = jax.random.fold_in(key, 22)
    counts = jax.random.randint(count_key, (HOLDERS,), max(SLOTS // 4, 1), SLOTS + 1)
    full = jax.random.randint(full_key, (), 0, HOLDERS)
    return jnp.where(jnp.arange(HOLDERS) == full, SLOTS, counts).astype(jnp.int32)


def touch_ends(values, own_key, low, largest):
    shape = values.shape
    spot = [jax.random.randint(jax.random.fold_in(own_key, axis), (), 0, shape[axis]) for axis in range(len(shape))]
    values = values.at[tuple(spot)].set(low)
    longest = shape.index(max(shape))
    spot[longest] = (spot[longest] + 1) % shape[longest]
    return values.at[tuple(spot)].set(largest)


def levels(rng, extent, split, smallest, largest):
    def one(dim, blocks):
        draws = jax.random.uniform(jax.random.fold_in(jax.random.fold_in(rng, 6), dim), (blocks,), jnp.float32, smallest / len(split), largest / len(split))
        return jnp.repeat(jnp.exp(draws), extent[dim] // blocks).reshape((-1,) + (1,) * (len(extent) - dim - 1))

    factor_of = one(*split[0])
    for cut in split[1:]:
        factor_of = factor_of * one(*cut)
    return factor_of


def centred(own_key, dims, scale, most, shards=(), held_as=jnp.bfloat16):
    values = jax.random.normal(own_key, dims, jnp.float32) * scale
    if len(shards) > 0:
        values = levels(own_key, dims, shards, -0.22, 0.18) * values
    return jnp.clip(values, min=-most, max=most).astype(held_as)


def setup_inputs(seed: int = 0) -> dict:
    arg_keys = jax.random.split(jax.random.key(seed), 15)
    log_depth = centred(arg_keys[0], (IMAGES, PIX), 0.3, 1.5, ((0, 32),), jnp.float32)
    depth_m = centred(arg_keys[1], (IMAGES, PIX), 0.001, 0.006, ((0, 32),), jnp.float32)
    depth_v = jnp.clip(jnp.exp(math.log(9.999999747378752e-06) - 4.6051701 * jax.random.uniform(arg_keys[2], (IMAGES, PIX), jnp.float32) ** levels(arg_keys[2], (IMAGES, PIX), ((0, 32),), -0.2, 0.2)), 1.0000000116860974e-07, 9.999999747378752e-06)
    image_params = centred(arg_keys[3], (7, IMAGES), 0.3, 1.5, ((1, 32),), jnp.float32)
    image_m = centred(arg_keys[4], (7, IMAGES), 1.0, 6.0, ((1, 32),), jnp.float32)
    image_v = jnp.clip(jnp.exp(math.log(10.0) - 4.6051702 * jax.random.uniform(arg_keys[5], (7, IMAGES), jnp.float32) ** levels(arg_keys[5], (7, IMAGES), ((1, 32),), -0.2, 0.2)), 0.1, 10.0)
    pair_points = centred(arg_keys[6], (PAIRS, 2, 3, PIX), 1.0, 6.0, ((0, 32),))
    pair_conf = jnp.clip(jnp.exp(math.log(5.0) - 1.609438 * jax.random.uniform(arg_keys[7], (PAIRS, 2, PIX), jnp.float32) ** levels(arg_keys[7], (PAIRS, 2, PIX), ((0, 32),), -0.2, 0.2)), 1.0, 5.0).astype(jnp.bfloat16)
    pair_params = centred(arg_keys[8], (7, PAIRS), 0.3, 1.5, ((1, 32),), jnp.float32)
    pair_m = centred(arg_keys[9], (7, PAIRS), 1.0, 6.0, ((1, 32),), jnp.float32)
    pair_v = jnp.clip(jnp.exp(math.log(10.0) - 4.6051702 * jax.random.uniform(arg_keys[10], (7, PAIRS), jnp.float32) ** levels(arg_keys[10], (7, PAIRS), ((1, 32),), -0.2, 0.2)), 0.1, 10.0)
    fetch = touch_ends(jax.random.randint(arg_keys[11], (HOLDERS, 2 * REACH + 1), 0, IMG_DEV), jax.random.fold_in(arg_keys[11], 1), 0, IMG_DEV - 1).astype(jnp.int32)
    pair_sides = draw_pair_sides(jax.random.fold_in(arg_keys[14], 71), 0)
    pair_count = draw_pair_count(jax.random.fold_in(arg_keys[14], 71), 0)
    return dict(log_depth=log_depth, depth_m=depth_m, depth_v=depth_v, image_params=image_params, image_m=image_m, image_v=image_v, pair_points=pair_points, pair_conf=pair_conf, pair_params=pair_params, pair_m=pair_m, pair_v=pair_v, fetch=fetch, pair_sides=pair_sides, pair_count=pair_count)


focal_base = 100.0
learn_rate = 0.05
beta_one = 0.9
beta_two = 0.999
adam_epsilon = 1e-08
adam_start = 20

def rotation(vector):
    xval, yval, zval = (vector[0], vector[1], vector[2])
    scale = 1.0 / (1.0 + xval * xval + yval * yval + zval * zval)
    return [[(1.0 + xval * xval - yval * yval - zval * zval) * scale, 2.0 * (xval * yval - zval) * scale, 2.0 * (xval * zval + yval) * scale], [2.0 * (xval * yval + zval) * scale, (1.0 - xval * xval + yval * yval - zval * zval) * scale, 2.0 * (yval * zval - xval) * scale], [2.0 * (xval * zval - yval) * scale, 2.0 * (yval * zval + xval) * scale, (1.0 - xval * xval - yval * yval + zval * zval) * scale]]

def residual_loss(depth_terms, image_terms, pair_terms, points, confidence, weight):
    total = depth_terms.shape[1]
    position = jnp.arange(total, dtype=jnp.int32)
    centre = (IMG_SIDE - 1) / 2.0
    column_pos = (position % IMG_SIDE).astype(jnp.float32) - centre
    row_pos = (position // IMG_SIDE).astype(jnp.float32) - centre
    focal = focal_base * jnp.exp(image_terms[6])[:, None]
    depth = jnp.exp(depth_terms)
    camera = (depth * column_pos[None, :] / focal, depth * row_pos[None, :] / focal, depth)
    spin = rotation(image_terms[0:3])
    turn = rotation(pair_terms[0:3])
    scale = jnp.exp(pair_terms[6])[:, None]
    squared = jnp.zeros_like(depth)
    for axis_id in range(3):
        world = spin[axis_id][0][:, None] * camera[0] + spin[axis_id][1][:, None] * camera[1] + spin[axis_id][2][:, None] * camera[2] + image_terms[3 + axis_id][:, None]
        target = scale * (turn[axis_id][0][:, None] * points[:, 0] + turn[axis_id][1][:, None] * points[:, 1] + turn[axis_id][2][:, None] * points[:, 2] + pair_terms[3 + axis_id][:, None])
        squared = squared + (world - target) * (world - target)
    per_term = lax.optimization_barrier(jnp.mean(confidence * squared, axis=1))
    return jnp.sum(weight * per_term)

def adam_step(param, grad, moment, second, count):
    moment = beta_one * moment + (1.0 - beta_one) * grad
    second = beta_two * second + (1.0 - beta_two) * grad * grad
    fix_one = 1.0 - beta_one ** count
    fix_two = 1.0 - beta_two ** count
    param = param - learn_rate * (moment / fix_one) / (jnp.sqrt(second / fix_two) + adam_epsilon)
    return (param, moment, second)

def reference(log_depth, depth_m, depth_v, image_params, image_m, image_v, pair_points, pair_conf, pair_params, pair_m, pair_v, fetch, pair_sides, pair_count):
    width_k = 2 * REACH + 1
    points_all = pair_points.reshape(HOLDERS, SLOTS, 2, 3, PIX)
    conf_all = pair_conf.reshape(HOLDERS, SLOTS, 2, PIX)
    sides_all = pair_sides.reshape(HOLDERS, SLOTS, 2)
    holder_ids = jnp.arange(HOLDERS, dtype=jnp.int32)
    window_pos = jnp.arange(width_k, dtype=jnp.int32)
    offsets = jnp.where(window_pos < 2 * REACH, window_pos - REACH, HOLDERS // 2).astype(jnp.int32)
    for step_id in range(ITERS):
        depth_used = lax.optimization_barrier(log_depth.astype(jnp.bfloat16)).astype(jnp.float32)
        params_used = lax.optimization_barrier(image_params.astype(jnp.bfloat16)).astype(jnp.float32)
        pair_blocks = pair_params.reshape(7, HOLDERS, SLOTS).transpose(1, 0, 2)

        def holder_step(carry, inputs):
            grad_depth, grad_params = carry
            holder, points, confidence, pair_block, fetch_row, sides, count = inputs
            owners = ((holder + offsets) % HOLDERS).astype(jnp.int32)
            image_ids = (owners * IMG_DEV + fetch_row).astype(jnp.int32)
            flat_ids = image_ids[sides.reshape(-1)]
            depth_terms = depth_used[flat_ids]
            image_terms = params_used[:, flat_ids]
            live = (jnp.arange(SLOTS, dtype=jnp.int32) < count).astype(jnp.float32)
            weight = jnp.repeat(live, 2)
            points_flat = points.reshape(2 * SLOTS, 3, PIX).astype(jnp.float32)
            conf_flat = confidence.reshape(2 * SLOTS, PIX).astype(jnp.float32)

            def loss_of(depth_in, params_in, pair_in):
                return residual_loss(depth_in, params_in, jnp.repeat(pair_in, 2, axis=1), points_flat, conf_flat, weight)
            value, pullback = jax.vjp(loss_of, depth_terms, image_terms, pair_block)
            grad_terms, grad_image, grad_pair = pullback(jnp.float32(1.0))
            grad_depth = grad_depth.at[flat_ids].add(grad_terms)
            grad_params = grad_params.at[:, flat_ids].add(grad_image)
            return ((grad_depth, grad_params), grad_pair)
        start = (jnp.zeros((IMAGES, PIX), jnp.float32), jnp.zeros((7, IMAGES), jnp.float32))
        (grad_depth, grad_params), grad_pairs = lax.scan(holder_step, start, (holder_ids, points_all, conf_all, pair_blocks, fetch, sides_all, pair_count))
        grad_pair = grad_pairs.transpose(1, 0, 2).reshape(7, PAIRS)
        count = adam_start + step_id + 1
        log_depth, depth_m, depth_v = adam_step(log_depth, grad_depth, depth_m, depth_v, count)
        image_params, image_m, image_v = adam_step(image_params, grad_params, image_m, image_v, count)
        pair_params, pair_m, pair_v = adam_step(pair_params, grad_pair, pair_m, pair_v, count)
    return (log_depth, image_params, pair_params)
```

```python
import functools

import jax
import jax.numpy as jnp
from jax import lax
from jax.experimental import pallas as pl
from jax.experimental.pallas import tpu as pltpu
from jax.sharding import PartitionSpec as P

IMG_SIDE = 112
REACH = 4
ITERS = 2
WIDTH = 2 * REACH + 1
LANES = 128

focal_base = 100.0
learn_rate = 0.05
beta_one = 0.9
beta_two = 0.999
adam_epsilon = 1e-08
adam_start = 20

MESH = pl.DeviceIdType.MESH
VMEM = pl.BlockSpec(memory_space=pltpu.VMEM)
VMEM_LIMIT = 48 * 1024 * 1024


def rotation(vector):
    xval, yval, zval = vector
    scale = 1.0 / (1.0 + xval * xval + yval * yval + zval * zval)
    return [
        [
            (1.0 + xval * xval - yval * yval - zval * zval) * scale,
            2.0 * (xval * yval - zval) * scale,
            2.0 * (xval * zval + yval) * scale,
        ],
        [
            2.0 * (xval * yval + zval) * scale,
            (1.0 - xval * xval + yval * yval - zval * zval) * scale,
            2.0 * (yval * zval - xval) * scale,
        ],
        [
            2.0 * (xval * zval - yval) * scale,
            2.0 * (yval * zval + xval) * scale,
            (1.0 - xval * xval - yval * yval + zval * zval) * scale,
        ],
    ]


def coefficients(image, pair):
    spin = rotation(image[0:3])
    turn = rotation(pair[0:3])
    scale = jnp.exp(pair[6])
    out = []
    for row in range(3):
        for col in range(3):
            out.append(scale * sum(spin[m][row] * turn[m][col] for m in range(3)))
    for row in range(3):
        out.append(sum(spin[m][row] * (scale * pair[3 + m] - image[3 + m]) for m in range(3)))
    out.append(jnp.exp(-image[6]) / focal_base)
    return out


def adam_step(param, grad, moment, second, count):
    moment = beta_one * moment + (1.0 - beta_one) * grad
    second = beta_two * second + (1.0 - beta_two) * grad * grad
    fix_one = 1.0 - beta_one**count
    fix_two = 1.0 - beta_two**count
    param = param - learn_rate * (moment / fix_one) / (jnp.sqrt(second / fix_two) + adam_epsilon)
    return (param, moment, second)


def shift(n, pos):
    return (n // 2) if pos == 2 * REACH else (pos - REACH) % n


def greet(n):
    me = lax.axis_index("dev")
    steps = sorted({shift(n, pos) for pos in range(WIDTH)} | {(n - shift(n, pos)) % n for pos in range(WIDTH)})
    steps = [step for step in steps if step != 0]
    barrier = pltpu.get_barrier_semaphore()
    for step in steps:
        pl.semaphore_signal(barrier, inc=1, device_id=(lax.rem(me + step, n),), device_id_type=MESH)
    pl.semaphore_wait(barrier, len(steps))


def exchange(n, to_owner, sent, got, send_sem, recv_sem):
    me = lax.axis_index("dev")
    copies = []
    for pos in range(WIDTH):
        step = shift(n, pos)
        if step == 0:
            continue
        target = lax.rem(me + (step if to_owner else n - step), n)
        copy = pltpu.make_async_remote_copy(
            src_ref=sent.at[pos],
            dst_ref=got.at[pos],
            send_sem=send_sem.at[pos],
            recv_sem=recv_sem.at[pos],
            device_id=(target,),
            device_id_type=MESH,
        )
        copy.start()
        copies.append(copy)
    got[REACH] = sent[REACH]
    for copy in copies:
        copy.wait()


def tile_loop(tiles, body):
    step = next(s for s in (7, 4, 2, 1) if tiles % s == 0)

    def several(outer, carry):
        for inner in range(step):
            body(outer * step + inner)
        return carry

    lax.fori_loop(0, tiles // step, several, 0)


def lane_tile(index):
    return pl.ds(pl.multiple_of(index * LANES, LANES), LANES)


def send_images(n, rows, tiles, depth_ref, par_ref, served, turned, sent, got, wide_ref, par_out, sems):
    count = depth_ref.shape[0]
    pad = (tiles // 8) * 8
    for img in range(count):
        turned[img * rows + pad : (img + 1) * rows, :] = jnp.zeros((rows - pad, LANES), jnp.float32)

    def turn(index):
        turned[pl.ds(index, count, stride=rows), :] = depth_ref[:, lane_tile(index)]

    tile_loop(tiles, turn)
    turned[pl.ds(tiles, count, stride=rows), :] = par_ref[...]
    for pos in range(WIDTH):
        total = jnp.zeros((rows, LANES), jnp.float32)
        for img in range(count):
            chosen = served[pos, 0:1, :] == img
            total = jnp.where(chosen, turned[img * rows : (img + 1) * rows, :], total)
        sent[pos] = total.astype(jnp.bfloat16)
    exchange(n, False, sent, got, *sems)
    for pos in range(WIDTH):
        turned[pos * rows : (pos + 1) * rows, :] = got[pos].astype(jnp.float32)
    turned[WIDTH * rows : 16 * rows, :] = jnp.zeros(((16 - WIDTH) * rows, LANES), jnp.float32)

    def back(index):
        for half in range(2):
            wide_ref[half * 8 : half * 8 + 8, lane_tile(index)] = turned[
                pl.ds(half * 8 * rows + index, 8, stride=rows), :
            ]

    tile_loop(tiles, back)
    for half in range(2):
        par_out[half * 8 : half * 8 + 8, :] = turned[pl.ds(half * 8 * rows + tiles, 8, stride=rows), :]


def return_grads(n, rows, tiles, count, grad_ref, pgrad_ref, served, turned, sent, got, sems, update, update_params):
    pad = (tiles // 8) * 8
    for pos in range(16):
        turned[pos * rows + pad : (pos + 1) * rows, :] = jnp.zeros((rows - pad, LANES), jnp.float32)

    def turn(index):
        for half in range(2):
            turned[pl.ds(half * 8 * rows + index, 8, stride=rows), :] = grad_ref[
                half * 8 : half * 8 + 8, lane_tile(index)
            ]

    tile_loop(tiles, turn)
    for half in range(2):
        turned[pl.ds(half * 8 * rows + tiles, 8, stride=rows), :] = pgrad_ref[half * 8 : half * 8 + 8, :]
    for pos in range(WIDTH):
        sent[pos] = turned[pos * rows : (pos + 1) * rows, :].astype(jnp.bfloat16)
    exchange(n, True, sent, got, *sems)
    for pos in range(WIDTH):
        turned[pos * rows : (pos + 1) * rows, :] = got[pos].astype(jnp.float32)
    local = lax.broadcasted_iota(jnp.int32, (count, LANES), 0)
    table = [(served[pos, 0:1, :] == local).astype(jnp.float32) for pos in range(WIDTH)]

    def combine(index):
        total = table[0] * turned[pl.ds(index, 1), :]
        for pos in range(1, WIDTH):
            total = total + table[pos] * turned[pl.ds(pos * rows + index, 1), :]
        return total

    tile_loop(tiles, lambda index: update(index, combine(index)))
    update_params(combine(tiles))


def first_kernel(n, rows, tiles, wanted, depth, par, wide, par_out, served, turned, sent, got, ss, rs, fs, fr):
    greet(n)
    exchange(n, True, wanted, served, fs, fr)
    send_images(n, rows, tiles, depth, par, served, turned, sent, got, wide, par_out, (ss, rs))


def middle_kernel(
    n, rows, tiles, count, grad, pgrad, served, depth, mom, sec, par, pmom, psec,
    wide, par_out, depth_n, mom_n, sec_n, par_n, pmom_n, psec_n,
    turned, sent, got, sent_b, got_b, ss, rs, bs, br,
):
    greet(n)

    def update(index, total):
        lane = lane_tile(index)
        depth_n[:, lane], mom_n[:, lane], sec_n[:, lane] = adam_step(
            depth[:, lane], total, mom[:, lane], sec[:, lane], count
        )

    def update_params(total):
        par_n[...], pmom_n[...], psec_n[...] = adam_step(par[...], total, pmom[...], psec[...], count)

    images = depth.shape[0]
    return_grads(n, rows, tiles, images, grad, pgrad, served, turned, sent_b, got_b, (bs, br), update, update_params)
    send_images(n, rows, tiles, depth_n, par_n, served, turned, sent, got, wide, par_out, (ss, rs))


def last_kernel(
    n, rows, tiles, count, grad, pgrad, served, depth, mom, sec, par, pmom, psec,
    depth_n, par_n, turned, sent, got, ss, rs,
):
    greet(n)

    def update(index, total):
        lane = lane_tile(index)
        depth_n[:, lane] = adam_step(depth[:, lane], total, mom[:, lane], sec[:, lane], count)[0]

    def update_params(total):
        par_n[...] = adam_step(par[...], total, pmom[...], psec[...], count)[0]

    images = depth.shape[0]
    return_grads(n, rows, tiles, images, grad, pgrad, served, turned, sent, got, (ss, rs), update, update_params)


def grad_kernel(chunks, pixels, pts, conf, wide, par, pair, pick, spread, cols, rows_, grad, pgrad, tgrad,
                coef, acc, gathered, held):
    step = pl.program_id(0)
    terms = pick.shape[0]
    width = wide.shape[1]

    def columns():
        mine = jnp.dot(pick[...], par[...].astype(jnp.bfloat16), preferred_element_type=jnp.float32)
        image = [mine[:, c : c + 1] for c in range(7)]
        other = [pair[:, c : c + 1] for c in range(7)]
        return image, other

    @pl.when(step == 0)
    def _():
        image, other = columns()
        for where, value in enumerate(coefficients(image, other)):
            coef[where] = jnp.broadcast_to(value, (terms, LANES))
        acc[...] = jnp.zeros_like(acc)

    gathered[...] = jnp.dot(pick[...], wide[...].astype(jnp.bfloat16), preferred_element_type=jnp.float32)
    for group in range(terms // 8):
        part = slice(group * 8, group * 8 + 8)
        cf = [coef[where, part, :] for where in range(13)]

        def tile(index, sums):
            lane = lane_tile(index)
            dep = jnp.exp(gathered[part, lane])
            point = [pts[j, part, lane] for j in range(3)]
            weight = conf[part, lane]
            fdep = dep * cf[12]
            camera = [fdep * cols[0:1, lane], fdep * rows_[0:1, lane], dep]
            fresh = []
            forces = []
            for i in range(3):
                aim = cf[3 * i] * point[0] + cf[3 * i + 1] * point[1] + (cf[3 * i + 2] * point[2] + cf[9 + i])
                forces.append(weight * (camera[i] - aim))
            for i in range(3):
                for j in range(3):
                    fresh.append(sums[3 * i + j] + forces[i] * point[j])
            for i in range(3):
                fresh.append(sums[9 + i] + forces[i])
            bend = forces[0] * camera[0] + forces[1] * camera[1]
            fresh.append(sums[12] + bend)
            held[part, lane] = bend + forces[2] * dep
            return tuple(fresh)

        def pair_of_tiles(index, sums):
            return tile(2 * index + 1, tile(2 * index, sums))

        sums = tuple(acc[where, part, :] for where in range(13))
        sums = lax.fori_loop(0, width // (2 * LANES), pair_of_tiles, sums)
        for where in range(13):
            acc[where, part, :] = sums[where]

    factor = 2.0 / pixels
    grad[...] = jnp.dot(
        spread[...], (held[...] * factor).astype(jnp.bfloat16), preferred_element_type=jnp.float32
    )

    @pl.when(step == chunks - 1)
    def _():
        image, other = columns()
        back = jax.vjp(coefficients, image, other)[1]
        total = [jnp.sum(acc[where], axis=1, keepdims=True) * factor for where in range(13)]
        focal = jnp.exp(image[6]) * focal_base
        image_g, other_g = back([-total[where] for where in range(12)] + [total[12] * focal])
        lane = lax.broadcasted_iota(jnp.int32, (terms, LANES), 1)
        whole = jnp.zeros((terms, LANES), jnp.float32)
        pairs = jnp.zeros((terms, LANES), jnp.float32)
        for c in range(7):
            whole = jnp.where(lane == c, image_g[c], whole)
            pairs = jnp.where(lane == c, other_g[c], pairs)
        pgrad[...] = jnp.dot(
            spread[...].astype(jnp.float32), whole, preferred_element_type=jnp.float32,
            precision=lax.Precision.HIGHEST,
        )
        tgrad[...] = pairs


def term_grads(points, conf, wide, par, pair, pick, spread, cols, rows_):
    _, terms, pixels = points.shape
    tiles = pixels // LANES
    chunks = next(c for c in (7, 4, 2, 1) if tiles % c == 0)
    width = pixels // chunks
    fixed = lambda shape: pl.BlockSpec(shape, lambda c: (0,) * len(shape))
    moving = lambda lead: pl.BlockSpec((lead, width), lambda c: (0, c))
    return pl.pallas_call(
        functools.partial(grad_kernel, chunks, pixels),
        grid=(chunks,),
        in_specs=[
            pl.BlockSpec((3, terms, width), lambda c: (0, 0, c)),
            moving(terms), moving(16), fixed((16, LANES)), fixed((terms, 8)),
            fixed((terms, 16)), fixed((16, terms)), moving(8), moving(8),
        ],
        out_specs=[moving(16), fixed((16, LANES)), fixed((terms, LANES))],
        out_shape=[
            jax.ShapeDtypeStruct((16, pixels), jnp.float32),
            jax.ShapeDtypeStruct((16, LANES), jnp.float32),
            jax.ShapeDtypeStruct((terms, LANES), jnp.float32),
        ],
        scratch_shapes=[
            pltpu.VMEM((13, terms, LANES), jnp.float32),
            pltpu.VMEM((13, terms, LANES), jnp.float32),
            pltpu.VMEM((terms, width), jnp.float32),
            pltpu.VMEM((terms, width), jnp.float32),
        ],
        compiler_params=pltpu.CompilerParams(vmem_limit_bytes=VMEM_LIMIT),
    )(points, conf, wide, par, pair, pick, spread, cols, rows_)


def on_device(
    log_depth, depth_m, depth_v, image_params, image_m, image_v,
    pair_points, pair_conf, pair_params, pair_m, pair_v, fetch, pair_sides, pair_count,
):
    n = lax.axis_size("dev")
    images, pixels = log_depth.shape
    slots = pair_sides.shape[0]
    terms = 2 * slots
    tiles = pixels // LANES
    rows = -(-(tiles + 1) // 16) * 16
    f32 = jnp.float32
    as_rows = lambda a: jnp.pad(a.T, ((0, 0), (0, LANES - 7)))
    par, pmom, psec = as_rows(image_params), as_rows(image_m), as_rows(image_v)
    wanted = jnp.broadcast_to(fetch[0][:, None, None], (WIDTH, 8, LANES))

    slot_shape = jax.ShapeDtypeStruct((WIDTH, 8, LANES), jnp.int32)
    big = jax.ShapeDtypeStruct((images, pixels), f32)
    small = jax.ShapeDtypeStruct((images, LANES), f32)
    wide_shape = [jax.ShapeDtypeStruct((16, pixels), f32), jax.ShapeDtypeStruct((16, LANES), f32)]
    message = pltpu.VMEM((WIDTH, rows, LANES), jnp.bfloat16)
    sem = pltpu.SemaphoreType.DMA((WIDTH,))
    turned = pltpu.VMEM((16 * rows, LANES), f32)

    def call(kernel, ident, outs, scratch, *args):
        return pl.pallas_call(
            kernel,
            out_shape=outs,
            in_specs=[VMEM] * len(args),
            out_specs=[VMEM] * len(outs),
            scratch_shapes=scratch,
            compiler_params=pltpu.CompilerParams(
                collective_id=ident, has_side_effects=True, vmem_limit_bytes=VMEM_LIMIT
            ),
        )(*args)

    wide, wide_par, served = call(
        functools.partial(first_kernel, n, rows, tiles), 0, wide_shape + [slot_shape],
        [turned, message, message, sem, sem, sem, sem], wanted, log_depth, par,
    )

    live = (jnp.arange(slots, dtype=jnp.int32) < pair_count[0]).astype(f32)
    conf = (pair_conf.astype(f32) * live[:, None, None]).reshape(terms, pixels)
    points = pair_points.transpose(2, 0, 1, 3).astype(f32).reshape(3, terms, pixels)
    flat = pair_sides.reshape(-1)
    places = jnp.arange(16, dtype=jnp.int32)
    pick = (flat[:, None] == places[None, :]).astype(jnp.bfloat16)
    spread = (places[:, None] == flat[None, :]).astype(jnp.bfloat16)
    position = jnp.arange(pixels, dtype=jnp.int32)
    centre = (IMG_SIDE - 1) / 2.0
    cols = jnp.broadcast_to(((position % IMG_SIDE).astype(f32) - centre)[None, :], (8, pixels))
    rows_ = jnp.broadcast_to(((position // IMG_SIDE).astype(f32) - centre)[None, :], (8, pixels))

    for step_id in range(ITERS):
        pair = jnp.repeat(jnp.pad(pair_params.T, ((0, 0), (0, 1))), 2, axis=0)
        grad, pgrad, tgrad = term_grads(points, conf, wide, wide_par, pair, pick, spread, cols, rows_)
        grad_pair = tgrad[:, :7].reshape(slots, 2, 7).sum(axis=1).T
        count = adam_start + step_id + 1
        pair_params, pair_m, pair_v = adam_step(pair_params, grad_pair, pair_m, pair_v, count)
        args = (grad, pgrad, served, log_depth, depth_m, depth_v, par, pmom, psec)
        if step_id < ITERS - 1:
            wide, wide_par, log_depth, depth_m, depth_v, par, pmom, psec = call(
                functools.partial(middle_kernel, n, rows, tiles, count), 1 + step_id,
                wide_shape + [big, big, big, small, small, small],
                [turned, message, message, message, message, sem, sem, sem, sem], *args,
            )
        else:
            log_depth, par = call(
                functools.partial(last_kernel, n, rows, tiles, count), 1 + step_id, [big, small],
                [turned, message, message, sem, sem], *args,
            )
    return (log_depth, par[:, :7].T, pair_params)


def solution(mesh):
    return jax.shard_map(
        on_device,
        mesh=mesh,
        in_specs=(
            P("dev", None),
            P("dev", None),
            P("dev", None),
            P(None, "dev"),
            P(None, "dev"),
            P(None, "dev"),
            P("dev", None, None, None),
            P("dev", None, None),
            P(None, "dev"),
            P(None, "dev"),
            P(None, "dev"),
            P("dev", None),
            P("dev", None),
            P("dev"),
        ),
        out_specs=(P("dev", None), P(None, "dev"), P(None, "dev")),
        check_vma=False,
    )
```

```python
import functools

import jax
import jax.numpy as jnp
from jax import lax
from jax.experimental import pallas as pl
from jax.experimental.pallas import tpu as pltpu
from jax.sharding import PartitionSpec as P

IMG_SIDE = 112
REACH = 4
ITERS = 2
WIDTH = 2 * REACH + 1
LANES = 128

focal_base = 100.0
learn_rate = 0.05
beta_one = 0.9
beta_two = 0.999
adam_epsilon = 1e-08
adam_start = 20

MESH = pl.DeviceIdType.MESH
VMEM = pl.BlockSpec(memory_space=pltpu.VMEM)
VMEM_LIMIT = 16 * 1024 * 1024


def rotation(vector):
    xval, yval, zval = vector
    scale = 1.0 / (1.0 + xval * xval + yval * yval + zval * zval)
    return [
        [
            (1.0 + xval * xval - yval * yval - zval * zval) * scale,
            2.0 * (xval * yval - zval) * scale,
            2.0 * (xval * zval + yval) * scale,
        ],
        [
            2.0 * (xval * yval + zval) * scale,
            (1.0 - xval * xval + yval * yval - zval * zval) * scale,
            2.0 * (yval * zval - xval) * scale,
        ],
        [
            2.0 * (xval * zval - yval) * scale,
            2.0 * (yval * zval + xval) * scale,
            (1.0 - xval * xval - yval * yval + zval * zval) * scale,
        ],
    ]


def coefficients(image, pair):
    spin = rotation(image[0:3])
    turn = rotation(pair[0:3])
    scale = jnp.exp(pair[6])
    out = []
    for row in range(3):
        for col in range(3):
            out.append(scale * sum(spin[m][row] * turn[m][col] for m in range(3)))
    for row in range(3):
        out.append(sum(spin[m][row] * (scale * pair[3 + m] - image[3 + m]) for m in range(3)))
    out.append(jnp.exp(-image[6]) / focal_base)
    return out


def adam_step(param, grad, moment, second, count):
    moment = beta_one * moment + (1.0 - beta_one) * grad
    second = beta_two * second + (1.0 - beta_two) * grad * grad
    fix_one = 1.0 - beta_one**count
    fix_two = 1.0 - beta_two**count
    param = param - learn_rate * (moment / fix_one) / (jnp.sqrt(second / fix_two) + adam_epsilon)
    return (param, moment, second)


def shift(n, pos):
    return (n // 2) if pos == 2 * REACH else (pos - REACH) % n


def partners(n):
    steps = {shift(n, pos) for pos in range(WIDTH)} | {(n - shift(n, pos)) % n for pos in range(WIDTH)}
    return sorted(steps - {0})


def greet(n):
    me = lax.axis_index("dev")
    barrier = pltpu.get_barrier_semaphore()
    for step in partners(n):
        pl.semaphore_signal(barrier, inc=1, device_id=(lax.rem(me + step, n),), device_id_type=MESH)


def await_partners(n):
    pl.semaphore_wait(pltpu.get_barrier_semaphore(), len(partners(n)))


ORDER = [2 * REACH] + sorted(range(2 * REACH), key=lambda pos: -abs(pos - REACH))


def send(n, to_owner, pos, sent, got, sems):
    me = lax.axis_index("dev")
    step = shift(n, pos)
    if step == 0:
        got[pos] = sent[pos]
        return None
    target = lax.rem(me + (step if to_owner else n - step), n)
    copy = pltpu.make_async_remote_copy(
        src_ref=sent.at[pos],
        dst_ref=got.at[pos],
        send_sem=sems[0].at[pos],
        recv_sem=sems[1].at[pos],
        device_id=(target,),
        device_id_type=MESH,
    )
    copy.start()
    return copy


def tile_loop(tiles, body):
    step = next(s for s in (7, 4, 2, 1) if tiles % s == 0)

    def several(outer, carry):
        for inner in range(step):
            body(outer * step + inner)
        return carry

    lax.fori_loop(0, tiles // step, several, 0)


def lane_tile(index):
    return pl.ds(pl.multiple_of(index * LANES, LANES), LANES)


def turn_images(rows, tiles, depth_ref, par_ref, turned):
    count = depth_ref.shape[0]
    pad = (tiles // 8) * 8
    for img in range(count):
        turned[img * rows + pad : (img + 1) * rows, :] = jnp.zeros((rows - pad, LANES), jnp.float32)

    def turn(index):
        turned[pl.ds(index, count, stride=rows), :] = depth_ref[:, lane_tile(index)]

    tile_loop(tiles, turn)
    turned[pl.ds(tiles, count, stride=rows), :] = par_ref[...]


def send_images(n, rows, tiles, count, served, turned, sent, got, wide_ref, par_out, sems):
    copies = []
    for pos in ORDER:
        total = turned[0:rows, :]
        for img in range(1, count):
            chosen = served[pos, 0:1, :] == img
            total = jnp.where(chosen, turned[img * rows : (img + 1) * rows, :], total)
        sent[pos] = total.astype(jnp.bfloat16)
        copies.append((pos, send(n, False, pos, sent, got, sems)))
    for pos, copy in copies[::-1]:
        if copy is not None:
            copy.wait()
        turned[pos * rows : (pos + 1) * rows, :] = got[pos].astype(jnp.float32)
    turned[WIDTH * rows : 16 * rows, :] = jnp.zeros(((16 - WIDTH) * rows, LANES), jnp.float32)

    def back(index):
        for half in range(2):
            wide_ref[half * 8 : half * 8 + 8, lane_tile(index)] = turned[
                pl.ds(half * 8 * rows + index, 8, stride=rows), :
            ]

    tile_loop(tiles, back)
    for half in range(2):
        par_out[half * 8 : half * 8 + 8, :] = turned[pl.ds(half * 8 * rows + tiles, 8, stride=rows), :]


def return_grads(n, rows, tiles, count, grad_ref, pgrad_ref, served, turned, sent, got, sems, update, update_params):
    greet(n)
    pad = (tiles // 8) * 8
    for pos in range(16):
        turned[pos * rows + pad : (pos + 1) * rows, :] = jnp.zeros((rows - pad, LANES), jnp.float32)

    def turn(index):
        for half in range(2):
            turned[pl.ds(half * 8 * rows + index, 8, stride=rows), :] = grad_ref[
                half * 8 : half * 8 + 8, lane_tile(index)
            ]

    tile_loop(tiles, turn)
    for half in range(2):
        turned[pl.ds(half * 8 * rows + tiles, 8, stride=rows), :] = pgrad_ref[half * 8 : half * 8 + 8, :]
    await_partners(n)
    copies = []
    for pos in ORDER:
        sent[pos] = turned[pos * rows : (pos + 1) * rows, :].astype(jnp.bfloat16)
        copies.append((pos, send(n, True, pos, sent, got, sems)))
    for pos, copy in copies[::-1]:
        if copy is not None:
            copy.wait()
        turned[pos * rows : (pos + 1) * rows, :] = got[pos].astype(jnp.float32)
    local = lax.broadcasted_iota(jnp.int32, (count, LANES), 0)
    table = [(served[pos, 0:1, :] == local).astype(jnp.float32) for pos in range(WIDTH)]

    def combine(index):
        total = table[0] * turned[pl.ds(index, 1), :]
        for pos in range(1, WIDTH):
            total = total + table[pos] * turned[pl.ds(pos * rows + index, 1), :]
        return total

    tile_loop(tiles, lambda index: update(index, combine(index)))
    update_params(combine(tiles))


def first_kernel(n, rows, tiles, wanted, depth, par, wide, par_out, served, turned, sent, got, ss, rs, fs, fr):
    greet(n)
    await_partners(n)
    copies = [send(n, True, pos, wanted, served, (fs, fr)) for pos in ORDER]
    turn_images(rows, tiles, depth, par, turned)
    for copy in copies:
        if copy is not None:
            copy.wait()
    send_images(n, rows, tiles, depth.shape[0], served, turned, sent, got, wide, par_out, (ss, rs))


def middle_kernel(
    n, rows, tiles, count, grad, pgrad, served, depth, mom, sec, par, pmom, psec,
    wide, par_out, depth_n, mom_n, sec_n, par_n, pmom_n, psec_n,
    turned, sent, got, sent_b, got_b, ss, rs, bs, br,
):

    def update(index, total):
        lane = lane_tile(index)
        depth_n[:, lane], mom_n[:, lane], sec_n[:, lane] = adam_step(
            depth[:, lane], total, mom[:, lane], sec[:, lane], count
        )

    def update_params(total):
        par_n[...], pmom_n[...], psec_n[...] = adam_step(par[...], total, pmom[...], psec[...], count)

    images = depth.shape[0]
    return_grads(n, rows, tiles, images, grad, pgrad, served, turned, sent_b, got_b, (bs, br), update, update_params)
    turn_images(rows, tiles, depth_n, par_n, turned)
    send_images(n, rows, tiles, images, served, turned, sent, got, wide, par_out, (ss, rs))


def last_kernel(
    n, rows, tiles, count, grad, pgrad, served, depth, mom, sec, par, pmom, psec,
    depth_n, par_n, turned, sent, got, ss, rs,
):

    def update(index, total):
        lane = lane_tile(index)
        depth_n[:, lane] = adam_step(depth[:, lane], total, mom[:, lane], sec[:, lane], count)[0]

    def update_params(total):
        par_n[...] = adam_step(par[...], total, pmom[...], psec[...], count)[0]

    images = depth.shape[0]
    return_grads(n, rows, tiles, images, grad, pgrad, served, turned, sent, got, (ss, rs), update, update_params)


def grad_kernel(chunks, pixels, pts, conf, wide, par, pair, pick, spread, cols, rows_, grad, pgrad, tgrad,
                coef, acc, gathered, held):
    step = pl.program_id(0)
    terms = pick.shape[0]
    width = wide.shape[1]

    def columns():
        mine = jnp.dot(pick[...], par[...].astype(jnp.bfloat16), preferred_element_type=jnp.float32)
        image = [mine[:, c : c + 1] for c in range(7)]
        other = [pair[:, c : c + 1] for c in range(7)]
        return image, other

    @pl.when(step == 0)
    def _():
        image, other = columns()
        for where, value in enumerate(coefficients(image, other)):
            coef[where] = jnp.broadcast_to(value, (terms, LANES))
        acc[...] = jnp.zeros_like(acc)

    gathered[...] = jnp.exp(
        jnp.dot(pick[...], wide[...].astype(jnp.bfloat16), preferred_element_type=jnp.float32)
    )
    for group in range(terms // 8):
        part = slice(group * 8, group * 8 + 8)
        cf = [coef[where, part, :] for where in range(13)]

        def tile(index, sums):
            lane = slice(index * LANES, (index + 1) * LANES)
            dep = gathered[part, lane]
            point = [pts[j, part, lane] for j in range(3)]
            weight = conf[part, lane]
            fdep = dep * cf[12]
            camera = [fdep * cols[:, lane], fdep * rows_[:, lane], dep]
            fresh = []
            forces = []
            for i in range(3):
                aim = cf[3 * i] * point[0] + cf[3 * i + 1] * point[1] + (cf[3 * i + 2] * point[2] + cf[9 + i])
                forces.append(weight * (camera[i] - aim))
            for i in range(3):
                for j in range(3):
                    fresh.append(sums[3 * i + j] + forces[i] * point[j])
            for i in range(3):
                fresh.append(sums[9 + i] + forces[i])
            bend = forces[0] * camera[0] + forces[1] * camera[1]
            fresh.append(sums[12] + bend)
            held[part, lane] = bend + forces[2] * dep
            return tuple(fresh)

        sums = tuple(acc[where, part, :] for where in range(13))
        for index in range(width // LANES):
            sums = tile(index, sums)
        for where in range(13):
            acc[where, part, :] = sums[where]

    factor = 2.0 / pixels
    grad[...] = jnp.dot(
        spread[...], (held[...] * factor).astype(jnp.bfloat16), preferred_element_type=jnp.float32
    )

    @pl.when(step == chunks - 1)
    def _():
        image, other = columns()
        back = jax.vjp(coefficients, image, other)[1]
        total = [jnp.sum(acc[where], axis=1, keepdims=True) * factor for where in range(13)]
        focal = jnp.exp(image[6]) * focal_base
        image_g, other_g = back([-total[where] for where in range(12)] + [total[12] * focal])
        lane = lax.broadcasted_iota(jnp.int32, (terms, LANES), 1)
        whole = jnp.zeros((terms, LANES), jnp.float32)
        pairs = jnp.zeros((terms, LANES), jnp.float32)
        for c in range(7):
            whole = jnp.where(lane == c, image_g[c], whole)
            pairs = jnp.where(lane == c, other_g[c], pairs)
        pgrad[...] = jnp.dot(
            spread[...].astype(jnp.float32), whole, preferred_element_type=jnp.float32,
            precision=lax.Precision.HIGHEST,
        )
        tgrad[...] = pairs


def spread_kernel(raw_points, raw_conf, live, points, conf):
    for slot in range(raw_points.shape[0]):
        part = slice(2 * slot, 2 * slot + 2)
        for j in range(3):
            points[j, part, :] = raw_points[slot, j].astype(jnp.float32)
        conf[part, :] = raw_conf[slot].astype(jnp.float32) * live[part, 0:1]


def spread_pairs(pair_points, pair_conf, live):
    slots, _, _, pixels = pair_points.shape
    terms = 2 * slots
    tiles = pixels // LANES
    chunks = next(c for c in (7, 4, 2, 1) if tiles % c == 0)
    width = pixels // chunks
    return pl.pallas_call(
        spread_kernel,
        grid=(chunks,),
        in_specs=[
            pl.BlockSpec((slots, 3, 2, width), lambda c: (0, 0, 0, c)),
            pl.BlockSpec((slots, 2, width), lambda c: (0, 0, c)),
            pl.BlockSpec((terms, LANES), lambda c: (0, 0)),
        ],
        out_specs=[
            pl.BlockSpec((3, terms, width), lambda c: (0, 0, c)),
            pl.BlockSpec((terms, width), lambda c: (0, c)),
        ],
        out_shape=[
            jax.ShapeDtypeStruct((3, terms, pixels), jnp.float32),
            jax.ShapeDtypeStruct((terms, pixels), jnp.float32),
        ],
        compiler_params=pltpu.CompilerParams(vmem_limit_bytes=VMEM_LIMIT),
    )(pair_points.transpose(0, 2, 1, 3), pair_conf, live)


def term_grads(points, conf, wide, par, pair, pick, spread, cols, rows_):
    _, terms, pixels = points.shape
    tiles = pixels // LANES
    chunks = next(c for c in (7, 4, 2, 1) if tiles % c == 0)
    width = pixels // chunks
    fixed = lambda shape: pl.BlockSpec(shape, lambda c: (0,) * len(shape))
    moving = lambda lead: pl.BlockSpec((lead, width), lambda c: (0, c))
    return pl.pallas_call(
        functools.partial(grad_kernel, chunks, pixels),
        grid=(chunks,),
        in_specs=[
            pl.BlockSpec((3, terms, width), lambda c: (0, 0, c)),
            moving(terms), moving(16), fixed((16, LANES)), fixed((terms, 8)),
            fixed((terms, 16)), fixed((16, terms)), moving(8), moving(8),
        ],
        out_specs=[moving(16), fixed((16, LANES)), fixed((terms, LANES))],
        out_shape=[
            jax.ShapeDtypeStruct((16, pixels), jnp.float32),
            jax.ShapeDtypeStruct((16, LANES), jnp.float32),
            jax.ShapeDtypeStruct((terms, LANES), jnp.float32),
        ],
        scratch_shapes=[
            pltpu.VMEM((13, terms, LANES), jnp.float32),
            pltpu.VMEM((13, terms, LANES), jnp.float32),
            pltpu.VMEM((terms, width), jnp.float32),
            pltpu.VMEM((terms, width), jnp.float32),
        ],
        compiler_params=pltpu.CompilerParams(vmem_limit_bytes=VMEM_LIMIT),
    )(points, conf, wide, par, pair, pick, spread, cols, rows_)


def on_device(
    log_depth, depth_m, depth_v, image_params, image_m, image_v,
    pair_points, pair_conf, pair_params, pair_m, pair_v, fetch, pair_sides, pair_count,
):
    n = lax.axis_size("dev")
    images, pixels = log_depth.shape
    slots = pair_sides.shape[0]
    terms = 2 * slots
    tiles = pixels // LANES
    rows = -(-(tiles + 1) // 16) * 16
    f32 = jnp.float32
    as_rows = lambda a: jnp.pad(a.T, ((0, 0), (0, LANES - 7)))
    par, pmom, psec = as_rows(image_params), as_rows(image_m), as_rows(image_v)
    wanted = jnp.broadcast_to(fetch[0][:, None, None], (WIDTH, 8, LANES))

    slot_shape = jax.ShapeDtypeStruct((WIDTH, 8, LANES), jnp.int32)
    big = jax.ShapeDtypeStruct((images, pixels), f32)
    small = jax.ShapeDtypeStruct((images, LANES), f32)
    wide_shape = [jax.ShapeDtypeStruct((16, pixels), f32), jax.ShapeDtypeStruct((16, LANES), f32)]
    message = pltpu.VMEM((WIDTH, rows, LANES), jnp.bfloat16)
    sem = pltpu.SemaphoreType.DMA((WIDTH,))
    turned = pltpu.VMEM((16 * rows, LANES), f32)

    def call(kernel, ident, outs, scratch, *args):
        return pl.pallas_call(
            kernel,
            out_shape=outs,
            in_specs=[VMEM] * len(args),
            out_specs=[VMEM] * len(outs),
            scratch_shapes=scratch,
            compiler_params=pltpu.CompilerParams(
                collective_id=ident, has_side_effects=True, vmem_limit_bytes=VMEM_LIMIT
            ),
        )(*args)

    wide, wide_par, served = call(
        functools.partial(first_kernel, n, rows, tiles), 0, wide_shape + [slot_shape],
        [turned, message, message, sem, sem, sem, sem], wanted, log_depth, par,
    )

    live = (jnp.arange(slots, dtype=jnp.int32) < pair_count[0]).astype(f32)
    live = jnp.broadcast_to(jnp.repeat(live, 2)[:, None], (terms, LANES))
    points, conf = spread_pairs(pair_points, pair_conf, live)
    flat = pair_sides.reshape(-1)
    places = jnp.arange(16, dtype=jnp.int32)
    pick = (flat[:, None] == places[None, :]).astype(jnp.bfloat16)
    spread = (places[:, None] == flat[None, :]).astype(jnp.bfloat16)
    position = jnp.arange(pixels, dtype=jnp.int32)
    centre = (IMG_SIDE - 1) / 2.0
    cols = jnp.broadcast_to(((position % IMG_SIDE).astype(f32) - centre)[None, :], (8, pixels))
    rows_ = jnp.broadcast_to(((position // IMG_SIDE).astype(f32) - centre)[None, :], (8, pixels))

    for step_id in range(ITERS):
        pair = jnp.repeat(jnp.pad(pair_params.T, ((0, 0), (0, 1))), 2, axis=0)
        grad, pgrad, tgrad = term_grads(points, conf, wide, wide_par, pair, pick, spread, cols, rows_)
        grad_pair = tgrad[:, :7].reshape(slots, 2, 7).sum(axis=1).T
        count = adam_start + step_id + 1
        pair_params, pair_m, pair_v = adam_step(pair_params, grad_pair, pair_m, pair_v, count)
        args = (grad, pgrad, served, log_depth, depth_m, depth_v, par, pmom, psec)
        if step_id < ITERS - 1:
            wide, wide_par, log_depth, depth_m, depth_v, par, pmom, psec = call(
                functools.partial(middle_kernel, n, rows, tiles, count), 1 + step_id,
                wide_shape + [big, big, big, small, small, small],
                [turned, message, message, message, message, sem, sem, sem, sem], *args,
            )
        else:
            log_depth, par = call(
                functools.partial(last_kernel, n, rows, tiles, count), 1 + step_id, [big, small],
                [turned, message, message, sem, sem], *args,
            )
    return (log_depth, par[:, :7].T, pair_params)


def solution(mesh):
    return jax.shard_map(
        on_device,
        mesh=mesh,
        in_specs=(
            P("dev", None),
            P("dev", None),
            P("dev", None),
            P(None, "dev"),
            P(None, "dev"),
            P(None, "dev"),
            P("dev", None, None, None),
            P("dev", None, None),
            P(None, "dev"),
            P(None, "dev"),
            P(None, "dev"),
            P("dev", None),
            P("dev", None),
            P("dev"),
        ),
        out_specs=(P("dev", None), P(None, "dev"), P(None, "dev")),
        check_vma=False,
    )
```

```python
import functools

import jax
import jax.numpy as jnp
from jax import lax
from jax.experimental import pallas as pl
from jax.experimental.pallas import tpu as pltpu
from jax.sharding import PartitionSpec as P

IMG_SIDE = 112
REACH = 4
ITERS = 2
WIDTH = 2 * REACH + 1
LANES = 128

focal_base = 100.0
learn_rate = 0.05
beta_one = 0.9
beta_two = 0.999
adam_epsilon = 1e-08
adam_start = 20

MESH = pl.DeviceIdType.MESH
VMEM = pl.BlockSpec(memory_space=pltpu.VMEM)
VMEM_LIMIT = 16 * 1024 * 1024
GRAD_VMEM_LIMIT = 48 * 1024 * 1024


def rotation(vector):
    xval, yval, zval = vector
    scale = 1.0 / (1.0 + xval * xval + yval * yval + zval * zval)
    return [
        [
            (1.0 + xval * xval - yval * yval - zval * zval) * scale,
            2.0 * (xval * yval - zval) * scale,
            2.0 * (xval * zval + yval) * scale,
        ],
        [
            2.0 * (xval * yval + zval) * scale,
            (1.0 - xval * xval + yval * yval - zval * zval) * scale,
            2.0 * (yval * zval - xval) * scale,
        ],
        [
            2.0 * (xval * zval - yval) * scale,
            2.0 * (yval * zval + xval) * scale,
            (1.0 - xval * xval - yval * yval + zval * zval) * scale,
        ],
    ]


def coefficients(image, pair):
    spin = rotation(image[0:3])
    turn = rotation(pair[0:3])
    scale = jnp.exp(pair[6])
    out = []
    for row in range(3):
        for col in range(3):
            out.append(scale * sum(spin[m][row] * turn[m][col] for m in range(3)))
    for row in range(3):
        out.append(sum(spin[m][row] * (scale * pair[3 + m] - image[3 + m]) for m in range(3)))
    out.append(jnp.exp(-image[6]) / focal_base)
    return out


def adam_step(param, grad, moment, second, count):
    moment = beta_one * moment + (1.0 - beta_one) * grad
    second = beta_two * second + (1.0 - beta_two) * grad * grad
    fix_one = 1.0 - beta_one**count
    fix_two = 1.0 - beta_two**count
    param = param - learn_rate * (moment / fix_one) / (jnp.sqrt(second / fix_two) + adam_epsilon)
    return (param, moment, second)


def shift(n, pos):
    return (n // 2) if pos == 2 * REACH else (pos - REACH) % n


def partners(n):
    steps = {shift(n, pos) for pos in range(WIDTH)} | {(n - shift(n, pos)) % n for pos in range(WIDTH)}
    return sorted(steps - {0})


def greet(n):
    me = lax.axis_index("dev")
    barrier = pltpu.get_barrier_semaphore()
    for step in partners(n):
        pl.semaphore_signal(barrier, inc=1, device_id=(lax.rem(me + step, n),), device_id_type=MESH)


def await_partners(n):
    pl.semaphore_wait(pltpu.get_barrier_semaphore(), len(partners(n)))


ORDER = [2 * REACH] + sorted(range(2 * REACH), key=lambda pos: -abs(pos - REACH))


def send(n, to_owner, pos, sent, got, sems):
    me = lax.axis_index("dev")
    step = shift(n, pos)
    if step == 0:
        got[pos] = sent[pos]
        return None
    target = lax.rem(me + (step if to_owner else n - step), n)
    copy = pltpu.make_async_remote_copy(
        src_ref=sent.at[pos],
        dst_ref=got.at[pos],
        send_sem=sems[0].at[pos],
        recv_sem=sems[1].at[pos],
        device_id=(target,),
        device_id_type=MESH,
    )
    copy.start()
    return copy


def bring(sources, targets, sem):
    copies = [pltpu.make_async_copy(a, b, sem.at[i]) for i, (a, b) in enumerate(zip(sources, targets))]
    for copy in copies:
        copy.start()
    return copies


def tile_loop(tiles, body):
    step = next(s for s in (7, 4, 2, 1) if tiles % s == 0)

    def several(outer, carry):
        for inner in range(step):
            body(outer * step + inner)
        return carry

    lax.fori_loop(0, tiles // step, several, 0)


def lane_tile(index):
    return pl.ds(pl.multiple_of(index * LANES, LANES), LANES)


def turn_images(rows, tiles, depth_ref, par_ref, turned):
    count = depth_ref.shape[0]
    pad = (tiles // 8) * 8
    for img in range(count):
        turned[img * rows + pad : (img + 1) * rows, :] = jnp.zeros((rows - pad, LANES), jnp.float32)

    def turn(index):
        turned[pl.ds(index, count, stride=rows), :] = depth_ref[:, lane_tile(index)]

    tile_loop(tiles, turn)
    turned[pl.ds(tiles, count, stride=rows), :] = par_ref[...]


def send_images(n, rows, tiles, count, served, turned, sent, got, wide_ref, par_out, sems):
    copies = []
    for pos in ORDER:
        total = turned[0:rows, :]
        for img in range(1, count):
            chosen = served[pos, 0:1, :] == img
            total = jnp.where(chosen, turned[img * rows : (img + 1) * rows, :], total)
        sent[pos] = total.astype(jnp.bfloat16)
        copies.append((pos, send(n, False, pos, sent, got, sems)))
    for pos, copy in copies[::-1]:
        if copy is not None:
            copy.wait()
        turned[pos * rows : (pos + 1) * rows, :] = got[pos].astype(jnp.float32)
    turned[WIDTH * rows : 16 * rows, :] = jnp.zeros(((16 - WIDTH) * rows, LANES), jnp.float32)

    def back(index):
        for half in range(2):
            wide_ref[half * 8 : half * 8 + 8, lane_tile(index)] = turned[
                pl.ds(half * 8 * rows + index, 8, stride=rows), :
            ]

    tile_loop(tiles, back)
    for half in range(2):
        par_out[half * 8 : half * 8 + 8, :] = turned[pl.ds(half * 8 * rows + tiles, 8, stride=rows), :]


def return_grads(n, rows, tiles, count, grad_ref, pgrad_ref, served, turned, sent, got, sems, update, update_params, loads):
    greet(n)
    pad = (tiles // 8) * 8
    for pos in range(16):
        turned[pos * rows + pad : (pos + 1) * rows, :] = jnp.zeros((rows - pad, LANES), jnp.float32)

    def turn(index):
        for half in range(2):
            turned[pl.ds(half * 8 * rows + index, 8, stride=rows), :] = grad_ref[
                half * 8 : half * 8 + 8, lane_tile(index)
            ]

    loads[0].wait()
    tile_loop(tiles, turn)
    for half in range(2):
        turned[pl.ds(half * 8 * rows + tiles, 8, stride=rows), :] = pgrad_ref[half * 8 : half * 8 + 8, :]
    await_partners(n)
    copies = []
    for pos in ORDER:
        sent[pos] = turned[pos * rows : (pos + 1) * rows, :].astype(jnp.bfloat16)
        copies.append((pos, send(n, True, pos, sent, got, sems)))
    for pos, copy in copies[::-1]:
        if copy is not None:
            copy.wait()
        turned[pos * rows : (pos + 1) * rows, :] = got[pos].astype(jnp.float32)
    local = lax.broadcasted_iota(jnp.int32, (count, LANES), 0)
    table = [(served[pos, 0:1, :] == local).astype(jnp.float32) for pos in range(WIDTH)]

    def combine(index):
        total = table[0] * turned[pl.ds(index, 1), :]
        for pos in range(1, WIDTH):
            total = total + table[pos] * turned[pl.ds(pos * rows + index, 1), :]
        return total

    for load in loads[1:]:
        load.wait()
    tile_loop(tiles, lambda index: update(index, combine(index)))
    update_params(combine(tiles))


def first_kernel(
    n, rows, tiles, wanted, par, depth_hbm, wide, par_out, served, turned, sent, got, ss, rs, fs, fr, depth, ls
):
    loads = bring([depth_hbm], [depth], ls)
    greet(n)
    await_partners(n)
    copies = [send(n, True, pos, wanted, served, (fs, fr)) for pos in ORDER]
    loads[0].wait()
    turn_images(rows, tiles, depth, par, turned)
    for copy in copies:
        if copy is not None:
            copy.wait()
    send_images(n, rows, tiles, depth.shape[0], served, turned, sent, got, wide, par_out, (ss, rs))


def middle_kernel(
    n, rows, tiles, count, pgrad, served, par, pmom, psec, grad_hbm, depth_hbm, mom_hbm, sec_hbm,
    wide, par_out, depth_n, mom_n, sec_n, par_n, pmom_n, psec_n,
    turned, sent, got, sent_b, got_b, ss, rs, bs, br, grad, depth, mom, sec, ls,
):
    loads = bring([grad_hbm, depth_hbm, mom_hbm, sec_hbm], [grad, depth, mom, sec], ls)

    def update(index, total):
        lane = lane_tile(index)
        depth_n[:, lane], mom_n[:, lane], sec_n[:, lane] = adam_step(
            depth[:, lane], total, mom[:, lane], sec[:, lane], count
        )

    def update_params(total):
        par_n[...], pmom_n[...], psec_n[...] = adam_step(par[...], total, pmom[...], psec[...], count)

    images = depth.shape[0]
    return_grads(n, rows, tiles, images, grad, pgrad, served, turned, sent_b, got_b, (bs, br), update, update_params, loads)
    turn_images(rows, tiles, depth_n, par_n, turned)
    send_images(n, rows, tiles, images, served, turned, sent, got, wide, par_out, (ss, rs))


def last_kernel(
    n, rows, tiles, count, pgrad, served, par, pmom, psec, grad_hbm, depth_hbm, mom_hbm, sec_hbm,
    depth_n, par_n, turned, sent, got, ss, rs, grad, depth, mom, sec, ls,
):
    loads = bring([grad_hbm, depth_hbm, mom_hbm, sec_hbm], [grad, depth, mom, sec], ls)

    def update(index, total):
        lane = lane_tile(index)
        depth_n[:, lane] = adam_step(depth[:, lane], total, mom[:, lane], sec[:, lane], count)[0]

    def update_params(total):
        par_n[...] = adam_step(par[...], total, pmom[...], psec[...], count)[0]

    images = depth.shape[0]
    return_grads(n, rows, tiles, images, grad, pgrad, served, turned, sent, got, (ss, rs), update, update_params, loads)


def grad_kernel(chunks, pixels, pts, conf, wide, par, pair, pick, spread, cols, rows_, grad, pgrad, tgrad,
                coef, acc, gathered, held):
    step = pl.program_id(0)
    terms = pick.shape[0]
    width = wide.shape[1]

    def columns():
        mine = jnp.dot(pick[...], par[...].astype(jnp.bfloat16), preferred_element_type=jnp.float32)
        image = [mine[:, c : c + 1] for c in range(7)]
        other = [pair[:, c : c + 1] for c in range(7)]
        return image, other

    @pl.when(step == 0)
    def _():
        image, other = columns()
        for where, value in enumerate(coefficients(image, other)):
            coef[where] = jnp.broadcast_to(value, (terms, LANES))
        acc[...] = jnp.zeros_like(acc)

    gathered[...] = jnp.exp(
        jnp.dot(pick[...], wide[...].astype(jnp.bfloat16), preferred_element_type=jnp.float32)
    )
    for group in range(terms // 8):
        part = slice(group * 8, group * 8 + 8)
        cf = [coef[where, part, :] for where in range(13)]

        def tile(index, sums):
            lane = slice(index * LANES, (index + 1) * LANES)
            dep = gathered[part, lane]
            point = [pts[j, part, lane] for j in range(3)]
            weight = conf[part, lane]
            fdep = dep * cf[12]
            camera = [fdep * cols[:, lane], fdep * rows_[:, lane], dep]
            fresh = []
            forces = []
            for i in range(3):
                aim = cf[3 * i] * point[0] + cf[3 * i + 1] * point[1] + (cf[3 * i + 2] * point[2] + cf[9 + i])
                forces.append(weight * (camera[i] - aim))
            for i in range(3):
                for j in range(3):
                    fresh.append(sums[3 * i + j] + forces[i] * point[j])
            for i in range(3):
                fresh.append(sums[9 + i] + forces[i])
            bend = forces[0] * camera[0] + forces[1] * camera[1]
            fresh.append(sums[12] + bend)
            held[part, lane] = bend + forces[2] * dep
            return tuple(fresh)

        sums = tuple(acc[where, part, :] for where in range(13))
        for index in range(width // LANES):
            sums = tile(index, sums)
        for where in range(13):
            acc[where, part, :] = sums[where]

    factor = 2.0 / pixels
    grad[...] = jnp.dot(
        spread[...], (held[...] * factor).astype(jnp.bfloat16), preferred_element_type=jnp.float32
    )

    @pl.when(step == chunks - 1)
    def _():
        image, other = columns()
        back = jax.vjp(coefficients, image, other)[1]
        total = [jnp.sum(acc[where], axis=1, keepdims=True) * factor for where in range(13)]
        focal = jnp.exp(image[6]) * focal_base
        image_g, other_g = back([-total[where] for where in range(12)] + [total[12] * focal])
        lane = lax.broadcasted_iota(jnp.int32, (terms, LANES), 1)
        whole = jnp.zeros((terms, LANES), jnp.float32)
        pairs = jnp.zeros((terms, LANES), jnp.float32)
        for c in range(7):
            whole = jnp.where(lane == c, image_g[c], whole)
            pairs = jnp.where(lane == c, other_g[c], pairs)
        pgrad[...] = jnp.dot(
            spread[...].astype(jnp.float32), whole, preferred_element_type=jnp.float32,
            precision=lax.Precision.HIGHEST,
        )
        tgrad[...] = pairs


def spread_kernel(raw_points, raw_conf, live, points, conf):
    for slot in range(raw_points.shape[0]):
        part = slice(2 * slot, 2 * slot + 2)
        for j in range(3):
            points[j, part, :] = raw_points[slot, j].astype(jnp.float32)
        conf[part, :] = raw_conf[slot].astype(jnp.float32) * live[part, 0:1]


def spread_pairs(pair_points, pair_conf, live):
    slots, _, _, pixels = pair_points.shape
    terms = 2 * slots
    tiles = pixels // LANES
    chunks = next(c for c in (7, 4, 2, 1) if tiles % c == 0)
    width = pixels // chunks
    return pl.pallas_call(
        spread_kernel,
        grid=(chunks,),
        in_specs=[
            pl.BlockSpec((slots, 3, 2, width), lambda c: (0, 0, 0, c)),
            pl.BlockSpec((slots, 2, width), lambda c: (0, 0, c)),
            pl.BlockSpec((terms, LANES), lambda c: (0, 0)),
        ],
        out_specs=[
            pl.BlockSpec((3, terms, width), lambda c: (0, 0, c)),
            pl.BlockSpec((terms, width), lambda c: (0, c)),
        ],
        out_shape=[
            jax.ShapeDtypeStruct((3, terms, pixels), jnp.float32),
            jax.ShapeDtypeStruct((terms, pixels), jnp.float32),
        ],
        compiler_params=pltpu.CompilerParams(vmem_limit_bytes=GRAD_VMEM_LIMIT),
    )(pair_points.transpose(0, 2, 1, 3), pair_conf, live)


def term_grads(points, conf, wide, par, pair, pick, spread, cols, rows_):
    _, terms, pixels = points.shape
    tiles = pixels // LANES
    chunks = next(c for c in (7, 4, 2, 1) if tiles % c == 0)
    width = pixels // chunks
    fixed = lambda shape: pl.BlockSpec(shape, lambda c: (0,) * len(shape))
    moving = lambda lead: pl.BlockSpec((lead, width), lambda c: (0, c))
    return pl.pallas_call(
        functools.partial(grad_kernel, chunks, pixels),
        grid=(chunks,),
        in_specs=[
            pl.BlockSpec((3, terms, width), lambda c: (0, 0, c)),
            moving(terms), moving(16), fixed((16, LANES)), fixed((terms, 8)),
            fixed((terms, 16)), fixed((16, terms)), moving(8), moving(8),
        ],
        out_specs=[moving(16), fixed((16, LANES)), fixed((terms, LANES))],
        out_shape=[
            jax.ShapeDtypeStruct((16, pixels), jnp.float32),
            jax.ShapeDtypeStruct((16, LANES), jnp.float32),
            jax.ShapeDtypeStruct((terms, LANES), jnp.float32),
        ],
        scratch_shapes=[
            pltpu.VMEM((13, terms, LANES), jnp.float32),
            pltpu.VMEM((13, terms, LANES), jnp.float32),
            pltpu.VMEM((terms, width), jnp.float32),
            pltpu.VMEM((terms, width), jnp.float32),
        ],
        compiler_params=pltpu.CompilerParams(vmem_limit_bytes=GRAD_VMEM_LIMIT),
    )(points, conf, wide, par, pair, pick, spread, cols, rows_)


def on_device(
    log_depth, depth_m, depth_v, image_params, image_m, image_v,
    pair_points, pair_conf, pair_params, pair_m, pair_v, fetch, pair_sides, pair_count,
):
    n = lax.axis_size("dev")
    images, pixels = log_depth.shape
    slots = pair_sides.shape[0]
    terms = 2 * slots
    tiles = pixels // LANES
    rows = -(-(tiles + 1) // 16) * 16
    f32 = jnp.float32
    as_rows = lambda a: jnp.pad(a.T, ((0, 0), (0, LANES - 7)))
    par, pmom, psec = as_rows(image_params), as_rows(image_m), as_rows(image_v)
    wanted = jnp.broadcast_to(fetch[0][:, None, None], (WIDTH, 8, LANES))

    slot_shape = jax.ShapeDtypeStruct((WIDTH, 8, LANES), jnp.int32)
    big = jax.ShapeDtypeStruct((images, pixels), f32)
    small = jax.ShapeDtypeStruct((images, LANES), f32)
    wide_shape = [jax.ShapeDtypeStruct((16, pixels), f32), jax.ShapeDtypeStruct((16, LANES), f32)]
    message = pltpu.VMEM((WIDTH, rows, LANES), jnp.bfloat16)
    sem = pltpu.SemaphoreType.DMA((WIDTH,))
    turned = pltpu.VMEM((16 * rows, LANES), f32)

    def call(kernel, ident, outs, scratch, args, far):
        return pl.pallas_call(
            kernel,
            out_shape=outs,
            in_specs=[VMEM] * len(args) + [pl.BlockSpec(memory_space=pl.ANY)] * len(far),
            out_specs=[VMEM] * len(outs),
            scratch_shapes=scratch
            + [pltpu.VMEM(a.shape, a.dtype) for a in far]
            + [pltpu.SemaphoreType.DMA((len(far),))],
            compiler_params=pltpu.CompilerParams(
                collective_id=ident, has_side_effects=True, vmem_limit_bytes=VMEM_LIMIT
            ),
        )(*args, *far)

    wide, wide_par, served = call(
        functools.partial(first_kernel, n, rows, tiles), 0, wide_shape + [slot_shape],
        [turned, message, message, sem, sem, sem, sem], (wanted, par), (log_depth,),
    )

    live = (jnp.arange(slots, dtype=jnp.int32) < pair_count[0]).astype(f32)
    live = jnp.broadcast_to(jnp.repeat(live, 2)[:, None], (terms, LANES))
    points, conf = spread_pairs(pair_points, pair_conf, live)
    flat = pair_sides.reshape(-1)
    places = jnp.arange(16, dtype=jnp.int32)
    pick = (flat[:, None] == places[None, :]).astype(jnp.bfloat16)
    spread = (places[:, None] == flat[None, :]).astype(jnp.bfloat16)
    position = jnp.arange(pixels, dtype=jnp.int32)
    centre = (IMG_SIDE - 1) / 2.0
    cols = jnp.broadcast_to(((position % IMG_SIDE).astype(f32) - centre)[None, :], (8, pixels))
    rows_ = jnp.broadcast_to(((position // IMG_SIDE).astype(f32) - centre)[None, :], (8, pixels))

    for step_id in range(ITERS):
        pair = jnp.repeat(jnp.pad(pair_params.T, ((0, 0), (0, 1))), 2, axis=0)
        grad, pgrad, tgrad = term_grads(points, conf, wide, wide_par, pair, pick, spread, cols, rows_)
        grad_pair = tgrad[:, :7].reshape(slots, 2, 7).sum(axis=1).T
        count = adam_start + step_id + 1
        pair_params, pair_m, pair_v = adam_step(pair_params, grad_pair, pair_m, pair_v, count)
        args = (pgrad, served, par, pmom, psec)
        far = (grad, log_depth, depth_m, depth_v)
        if step_id < ITERS - 1:
            wide, wide_par, log_depth, depth_m, depth_v, par, pmom, psec = call(
                functools.partial(middle_kernel, n, rows, tiles, count), 1 + step_id,
                wide_shape + [big, big, big, small, small, small],
                [turned, message, message, message, message, sem, sem, sem, sem], args, far,
            )
        else:
            log_depth, par = call(
                functools.partial(last_kernel, n, rows, tiles, count), 1 + step_id, [big, small],
                [turned, message, message, sem, sem], args, far,
            )
    return (log_depth, par[:, :7].T, pair_params)


def solution(mesh):
    return jax.shard_map(
        on_device,
        mesh=mesh,
        in_specs=(
            P("dev", None),
            P("dev", None),
            P("dev", None),
            P(None, "dev"),
            P(None, "dev"),
            P(None, "dev"),
            P("dev", None, None, None),
            P("dev", None, None),
            P(None, "dev"),
            P(None, "dev"),
            P(None, "dev"),
            P("dev", None),
            P("dev", None),
            P("dev"),
        ),
        out_specs=(P("dev", None), P(None, "dev"), P(None, "dev")),
        check_vma=False,
    )
```
